512 devices in a mesh: rows: 64 (over z, x_hi, core), feat: 8 (over y, x_lo).
Axes of the slice: x: 4 (x_hi: 2, x_lo: 2; x = x_hi * 2 + x_lo), y: 4, z: 16, core: 2. Of those that a mesh axis runs over, the one named last changes fastest.
Arguments:
- gradients: bfloat16 [65536, 8192], P('rows', 'feat'), may hold values from -2500 to 2500
- queries: bfloat16 [1024, 8192], P('rows', 'feat'), may hold values from -0.1875 to 0.1875
- loss_weight: float32 [65536], P('rows'), may hold values from 0.09 to 1
Outputs:
- standardized: bfloat16 [65536, 1024], P('rows', 'feat')
The draws below stay inside these ranges and needn't reach their ends.
All inputs are finite; a program needn't handle non-finite values.
Results may differ from the reference program's by a relative error of at most 0.019.
Values may be sent and summed in bfloat16 or wider, within the bound.
A program may use at most 64 MiB of HBM per device.

```python
import math
import jax
import jax.numpy as jnp
from jax import lax

K = 8192
QUERIES = 1024
ROW_DEV = 1024
TOTAL = 65536
N_FEAT = 8


def draw_gradients(key, part):
    key_rows = jax.random.fold_in(key, 11)
    key_cols = jax.random.fold_in(key, 12)
    key_mean = jax.random.fold_in(key, 13)
    key_noise = jax.random.fold_in(key, 14)
    key_tilt = jax.random.fold_in(key, 15)
    key_flip = jax.random.fold_in(key, 16)
    key_phase = jax.random.fold_in(key, 17)
    key_block = jax.random.fold_in(key, 18)
    block_count = TOTAL // ROW_DEV
    rows_uniform = jax.random.uniform(key_rows, (TOTAL, 1), jnp.float32)
    cols_uniform = jax.random.uniform(key_cols, (1, K), jnp.float32)
    tilt_uniform = jax.random.uniform(key_tilt, (TOTAL, 1), jnp.float32, -1.0, 1.0)
    column_shift = jax.random.truncated_normal(key_mean, -4.0, 4.0, (1, K), jnp.float32)
    position = jnp.arange(K, dtype=jnp.float32)[None, :] / K
    column_scale = jnp.exp(math.log(3.0) * position) * jnp.exp(math.log(2.0) * cols_uniform)
    flip_sign = (2 * jax.random.randint(key_flip, (), 0, 2) - 1).astype(jnp.float32)
    phase = jax.random.uniform(key_phase, (), jnp.float32, 0.0, 2.0 * math.pi)
    block_index = jnp.arange(block_count, dtype=jnp.int32)
    parity_sign = (1 - 2 * (block_index % 2)).astype(jnp.float32)
    block_place = (block_index.astype(jnp.float32) + 0.5) / block_count
    block_jitter = jax.random.uniform(key_block, (block_count,), jnp.float32, -1.0, 1.0)
    block_log = 0.6 * flip_sign * parity_sign + 0.6 * jnp.cos(2.0 * math.pi * block_place + phase) + 0.2 * block_jitter
    noise_level = jnp.repeat(jnp.exp(block_log), ROW_DEV, total_repeat_length=TOTAL)[:, None]
    noise = jax.random.truncated_normal(key_noise, -5.0, 5.0, (TOTAL, K), jnp.float32)
    row_scale = jnp.exp(math.log(10.0) * rows_uniform)
    shifted = noise_level * noise + 1.5 * column_shift
    tilt = jnp.exp(math.log(4.0) * tilt_uniform * (position - 0.5))
    return jnp.clip(row_scale * column_scale * tilt * shifted, -2500.0, 2500.0).astype(jnp.bfloat16)


def draw_loss_weight(key, part):
    position = jnp.arange(TOTAL, dtype=jnp.float32) / TOTAL
    trend = jnp.exp(math.log(3.0) * (position - 1.0))
    factor = jax.random.uniform(jax.random.fold_in(key, 21), (TOTAL,), jnp.float32, 0.3, 1.0)
    return (trend * factor).astype(jnp.float32)


def strengthened(result, rng, source, target, shards_of, factor):
    def block_of(dim):
        return (jnp.arange(result.shape[dim]) // (result.shape[dim] // shards_of)).reshape((-1,) + (1,) * (result.ndim - 1 - dim))

    one_side = jax.random.permutation(rng, shards_of)[block_of(target)]
    other_side = (block_of(target) + shards_of // 2) % shards_of
    return jnp.where((block_of(source) == one_side) | (block_of(source) == other_side), factor * result, result)


def block_scale(key, extent, split, low, high):
    factor_of = 1.0
    for dim, blocks in split:
        heights = jax.random.uniform(jax.random.fold_in(jax.random.fold_in(key, 6), dim), (blocks,), jnp.float32, low / len(split), high / len(split))
        factor_of = factor_of * jnp.repeat(jnp.exp(heights), extent[dim] // blocks).reshape((-1,) + (1,) * (len(extent) - 1 - dim))
    return factor_of


def noise_with(own_key, dims, deviation, reach, split, heavy, kind=jnp.bfloat16):
    array = deviation * jax.random.normal(own_key, dims, jnp.float32)
    if split:
        array = array * block_scale(own_key, dims, split, -0.22, 0.18)
    return jnp.clip(strengthened(array, jax.random.fold_in(own_key, 3), *heavy), -reach, reach).astype(kind)


def setup_inputs(seed: int = 0) -> dict:
    splits = jax.random.split(jax.random.key(seed), 4)
    gradients = draw_gradients(jax.random.fold_in(splits[3], 71), 0)
    queries = noise_with(splits[1], (QUERIES, K), K ** -0.5, 0.1875, ((0, 64), (1, 8)), (1, 0, 64, 4.0))
    loss_weight = draw_loss_weight(jax.random.fold_in(splits[3], 71), 0)
    return dict(gradients=gradients, queries=queries, loss_weight=loss_weight)


NORM_EPS = 1e-06
VAR_EPS = 1e-05

def reference(gradients, queries, loss_weight):
    column_width = K // N_FEAT
    squares = lax.optimization_barrier(jnp.sum(jnp.square(gradients.astype(jnp.float32)), axis=1))
    raw = jnp.zeros((TOTAL, QUERIES), jnp.float32)
    for block in range(N_FEAT):
        lower = block * column_width
        upper = lower + column_width
        partial_value = lax.dot_general(gradients[:, lower:upper], queries[:, lower:upper], (((1,), (1,)), ((), ())), preferred_element_type=jnp.float32)
        raw = raw + partial_value.astype(jnp.bfloat16).astype(jnp.float32)
    factor = loss_weight / jnp.sqrt(squares / K + NORM_EPS)
    scored = raw * factor[:, None]
    column_mean = lax.optimization_barrier(jnp.mean(scored, axis=0))
    centered = scored - column_mean[None, :]
    column_var = lax.optimization_barrier(jnp.mean(centered * centered, axis=0))
    return (centered * lax.rsqrt(column_var + VAR_EPS)[None, :]).astype(jnp.bfloat16)
```

```python
import functools
import jax
import jax.numpy as jnp
from jax import lax
from jax.experimental import pallas as pl
from jax.experimental.pallas import tpu as pltpu
from jax.sharding import PartitionSpec as P

NORM_EPS = 1e-06
VAR_EPS = 1e-05

NZ, NR, NF = 16, 64, 8
QB = 16
CHUNKS = 4
MESH = pl.DeviceIdType.MESH

FIRST, SECOND = (3, -3, 1, -1), (6, -6)
THIRD, LAST = (4, -4, 2, -2), (7, -7, 5, -5, 8)


def kernel(
    g_ref, q_ref, lw_ref, o_ref,
    qall, part, got, sq_mine, sq_got, scored, fac, stat_mine, stat_got,
    z_send, z_recv, x_send, x_recv, c_send, c_recv, d_send, d_recv,
    f_send, f_recv, s_send, s_recv, t_send, t_recv,
):
    r, f = lax.axis_index("rows"), lax.axis_index("feat")
    z, xh, c = r // 4, lax.rem(r // 2, 2), lax.rem(r, 2)
    rows = g_ref.shape[0]
    cols = g_ref.shape[1]

    def at(dz, xh_to, c_to):
        return (lax.rem(z + dz + NZ, NZ) * 4 + xh_to * 2 + c_to, f)

    def block(dz, xh_of, c_of):
        first = (lax.rem(z + dz + NZ, NZ) * 4 + xh_of * 2 + c_of) * QB
        return qall.at[pl.ds(pl.multiple_of(first, QB), QB)]

    def feat_peer(k):
        return (r, lax.rem(f + k, NF))

    barrier = pltpu.get_barrier_semaphore()
    greet = [at(d, xh, c) for d in (1, -1, 3, -3, 4 * c - 2)]
    greet += [at(0, 1 - xh, c), at(0, xh, 1 - c)]
    greet += [feat_peer(k) for k in range(1, NF)]
    for device in greet:
        pl.semaphore_signal(barrier, inc=1, device_id=device, device_id_type=MESH)

    lanes = 128
    for i in range(8):
        piece = rows // 8
        sums = jnp.zeros((piece, lanes), jnp.float32)
        for j in range(cols // lanes):
            v = g_ref[i * piece:(i + 1) * piece, j * lanes:(j + 1) * lanes].astype(jnp.float32)
            sums = sums + v * v
        sq_mine[:, i * piece:(i + 1) * piece] = jnp.sum(jnp.transpose(sums), axis=0, keepdims=True)
    block(0, xh, c)[...] = q_ref[...]

    pl.semaphore_wait(barrier, len(greet))

    sends = []

    def push(src, dst, ssem, rsem, device):
        copy = pltpu.make_async_remote_copy(
            src_ref=src, dst_ref=dst, send_sem=ssem, recv_sem=rsem,
            device_id=device, device_id_type=MESH)
        copy.start()
        sends.append(copy)

    def landed(dst, rsem):
        pltpu.make_async_remote_copy(
            src_ref=dst, dst_ref=dst, send_sem=z_send.at[0], recv_sem=rsem,
            device_id=at(0, xh, 1 - c), device_id_type=MESH).wait_recv()

    count = [0]

    def z_push(d, step):
        here = block(-d, xh, c)
        push(here, here, z_send.at[count[0]], z_recv.at[(d + step) % NZ], at(step, xh, c))
        count[0] += 1

    def share(d):
        here = block(-d, xh, c)
        push(here, here, x_send.at[d % NZ], x_recv.at[d % NZ], at(0, 1 - xh, c))
        push(here, here, c_send.at[d % NZ], c_recv.at[d % NZ], at(0, xh, 1 - c))

    def share_x(d):
        here = block(-d, 1 - xh, c)
        landed(here, x_recv.at[d % NZ])
        push(here, here, d_send.at[d % NZ], d_recv.at[d % NZ], at(0, xh, 1 - c))

    for step in (3, -3, 1, -1):
        z_push(0, step)
    share(0)
    for k in range(1, NF):
        push(sq_mine, sq_got.at[k - 1], s_send.at[k - 1], s_recv.at[k - 1], feat_peer(k))
    for d in FIRST:
        landed(block(-d, xh, c), z_recv.at[d % NZ])
        if d == 3:
            for step in (3, 1, -1):
                z_push(d, step)
        if d == -3:
            for step in (-3, -1, 1):
                z_push(d, step)
        share(d)
    share_x(0)
    for d in SECOND:
        landed(block(-d, xh, c), z_recv.at[d % NZ])
        z_push(d, 1)
        z_push(d, -1)
        if d == -6:
            turn = 1 - 2 * c
            here = block(-6 * turn, xh, c)
            push(here, here, z_send.at[count[0]], z_recv.at[8], at(2 * turn, xh, c))
            count[0] += 1
        share(d)
    for d in THIRD:
        landed(block(-d, xh, c), z_recv.at[d % NZ])
        share(d)
    for d in FIRST:
        share_x(d)

    total = sq_mine[...]
    for k in range(1, NF):
        landed(sq_got.at[k - 1], s_recv.at[k - 1])
        total = total + sq_got[k - 1]
    factor = lw_ref[...] / jnp.sqrt(total / (cols * NF) + NORM_EPS)
    fac[...] = jnp.transpose(jnp.broadcast_to(factor, (lanes, rows)))

    for d in LAST:
        landed(block(-d, xh, c), z_recv.at[d % NZ])
        share(d)
    for d in SECOND + THIRD + LAST:
        share_x(d)
    for d in (0,) + FIRST + SECOND + THIRD + LAST:
        landed(block(-d, xh, 1 - c), c_recv.at[d % NZ])
        landed(block(-d, 1 - xh, 1 - c), d_recv.at[d % NZ])

    size = rows // CHUNKS
    share_w = o_ref.shape[1]

    def chunk_copy(i, k):
        span = pl.ds(pl.multiple_of(i * size, size), size)
        to = lax.rem(f + k, NF)
        return pltpu.make_async_remote_copy(
            src_ref=part.at[to, span], dst_ref=got.at[k - 1, span],
            send_sem=f_send.at[i, k - 1], recv_sem=f_recv.at[i, k - 1],
            device_id=(r, to), device_id_type=MESH)

    @pl.loop(0, CHUNKS)
    def _(i):
        span = pl.ds(pl.multiple_of(i * size, size), size)
        product = lax.dot_general(g_ref[span, :], qall[...], (((1,), (1,)), ((), ())),
                                  preferred_element_type=jnp.float32)
        for b in range(NF):
            part[b, span, :] = product[:, b * share_w:(b + 1) * share_w].astype(jnp.bfloat16)
        for k in range(1, NF):
            chunk_copy(i, k).start()

    def take(i, column_sum):
        span = pl.ds(pl.multiple_of(i * size, size), size)
        raw = part[f, span, :].astype(jnp.float32)
        for k in range(1, NF):
            chunk_copy(i, k).wait_recv()
            raw = raw + got[k - 1, span, :].astype(jnp.float32)
        value = raw * fac[span, :]
        scored[span, :] = value
        return column_sum + jnp.sum(value, axis=0, keepdims=True)

    column_sum = lax.fori_loop(0, CHUNKS, take, jnp.zeros((1, share_w), jnp.float32))
    own_mean = column_sum / rows
    off = scored[...] - own_mean
    stat_mine[0:1, :] = own_mean
    stat_mine[1:2, :] = jnp.sum(off * off, axis=0, keepdims=True)

    def stat_copy(i):
        return pltpu.make_async_remote_copy(
            src_ref=stat_mine, dst_ref=stat_got.at[i - 1],
            send_sem=t_send.at[i - 1], recv_sem=t_recv.at[i - 1],
            device_id=(lax.rem(r + i, NR), f), device_id_type=MESH)

    @pl.loop(1, NR)
    def _(i):
        stat_copy(i).start()

    @pl.loop(1, NR)
    def _(i):
        stat_copy(i).wait_recv()

    means = stat_got[:, 0, :]
    mean = (jnp.sum(means, axis=0, keepdims=True) + own_mean) / NR
    apart = means - mean
    own_apart = own_mean - mean
    spread = jnp.sum(stat_got[:, 1, :], axis=0, keepdims=True) + stat_mine[1:2, :]
    spread = spread + rows * (jnp.sum(apart * apart, axis=0, keepdims=True) + own_apart * own_apart)
    scale = lax.rsqrt(spread / (rows * NR) + VAR_EPS)
    o_ref[...] = ((scored[...] - mean) * scale).astype(o_ref.dtype)

    for copy in sends:
        copy.wait_send()

    @pl.loop(0, CHUNKS)
    def _(i):
        for k in range(1, NF):
            chunk_copy(i, k).wait_send()

    @pl.loop(1, NR)
    def _(i):
        stat_copy(i).wait_send()


def body(gradients, queries, loss_weight):
    rows, cols = gradients.shape
    width = queries.shape[0] * NR // NF
    dma = pltpu.SemaphoreType.DMA
    return pl.pallas_call(
        kernel,
        out_shape=jax.ShapeDtypeStruct((rows, width), jnp.bfloat16),
        in_specs=[pl.BlockSpec(memory_space=pltpu.VMEM)] * 3,
        out_specs=pl.BlockSpec(memory_space=pltpu.VMEM),
        scratch_shapes=[
            pltpu.VMEM((NR * QB, cols), jnp.bfloat16),
            pltpu.VMEM((NF, rows, width), jnp.bfloat16),
            pltpu.VMEM((NF - 1, rows, width), jnp.bfloat16),
            pltpu.VMEM((1, rows), jnp.float32),
            pltpu.VMEM((NF - 1, 1, rows), jnp.float32),
            pltpu.VMEM((rows, width), jnp.float32),
            pltpu.VMEM((rows, width), jnp.float32),
            pltpu.VMEM((2, width), jnp.float32),
            pltpu.VMEM((NR - 1, 2, width), jnp.float32),
            dma((NZ - 1,)), dma((NZ,)), dma((NZ,)), dma((NZ,)),
            dma((NZ,)), dma((NZ,)), dma((NZ,)), dma((NZ,)),
            dma((CHUNKS, NF - 1)), dma((CHUNKS, NF - 1)),
            dma((NF - 1,)), dma((NF - 1,)), dma((NR - 1,)), dma((NR - 1,)),
        ],
        compiler_params=pltpu.CompilerParams(
            collective_id=0, has_side_effects=True, vmem_limit_bytes=40 * 2**20),
        cost_estimate=pl.CostEstimate(
            flops=2 * rows * NR * QB * cols, bytes_accessed=2 * rows * (cols + width), transcendentals=0),
        name="scores",
    )(gradients, queries, loss_weight.reshape(1, rows))


def solution(mesh):
    in_specs = (P("rows", "feat"), P("rows", "feat"), P("rows"))
    out_specs = P("rows", "feat")
    return jax.shard_map(body, mesh=mesh, in_specs=in_specs, out_specs=out_specs, check_vma=False)
```

```python
import jax
import jax.numpy as jnp
from jax import lax
from jax.experimental import pallas as pl
from jax.experimental.pallas import tpu as pltpu
from jax.sharding import PartitionSpec as P

NORM_EPS = 1e-06
VAR_EPS = 1e-05

NZ, NR, NF, NY = 16, 64, 8, 4
QB = 16
CHUNKS = 4
LANES = 128
MESH = pl.DeviceIdType.MESH

FIRST, SECOND = (3, -3, 1, -1), (6, -6)
THIRD, LAST = (4, -4, 2, -2), (7, -7, 5, -5, 8)


def kernel(
    g_hbm, q_hbm, lw_hbm, o_ref,
    g, qall, lw, pa, pb, a_got, a_out, a_own, ax_got, bx_got, b_out, b_own, by_got,
    sq_mine, sq_got, sq_pair, sq_far, factor, scored, stat_mine, stat_got,
    l_sem, z_send, z_recv, x_send, x_recv, c_send, c_recv, d_send, d_recv,
    ay_send, ay_recv, ax_send, ax_recv, bx_send, bx_recv, by_send, by_recv,
    s_send, s_recv, t_send, t_recv,
):
    r, f = lax.axis_index("rows"), lax.axis_index("feat")
    z, xh, c = r // 4, lax.rem(r // 2, 2), lax.rem(r, 2)
    y, xl = f // 2, lax.rem(f, 2)
    rows, cols = g.shape
    size = rows // CHUNKS
    half = qall.shape[0] // 2
    per = half // NF

    def at(dz, xh_to, c_to):
        return (lax.rem(z + dz + NZ, NZ) * 4 + xh_to * 2 + c_to, f)

    def y_peer(k):
        return (r, lax.rem(y + k, NY) * 2 + xl)

    x_peer = (r, y * 2 + 1 - xl)

    def block(dz, xh_of, c_of):
        first = xh_of * half + lax.rem(z + dz + NZ, NZ) * (2 * QB) + c_of * QB
        return qall.at[pl.ds(pl.multiple_of(first, QB), QB)]

    loads = [
        pltpu.make_async_copy(q_hbm, block(0, xh, c), l_sem.at[0]),
        pltpu.make_async_copy(g_hbm, g, l_sem.at[1]),
        pltpu.make_async_copy(lw_hbm, lw, l_sem.at[2]),
    ]
    for load in loads:
        load.start()

    barrier = pltpu.get_barrier_semaphore()
    greet = [at(d, xh, c) for d in (3, -3, 4 * c - 2, 1, -1)]
    greet += [at(0, 1 - xh, c), at(0, xh, 1 - c), x_peer]
    greet += [y_peer(k) for k in range(1, NY)]
    for device in greet:
        pl.semaphore_signal(barrier, inc=1, device_id=device, device_id_type=MESH)
    loads[0].wait()
    pl.semaphore_wait(barrier, len(greet))

    sends = []

    def push(src, dst, ssem, rsem, device):
        copy = pltpu.make_async_remote_copy(
            src_ref=src, dst_ref=dst, send_sem=ssem, recv_sem=rsem,
            device_id=device, device_id_type=MESH)
        copy.start()
        sends.append(copy)

    def landed(dst, rsem):
        pltpu.make_async_remote_copy(
            src_ref=dst, dst_ref=dst, send_sem=z_send.at[0], recv_sem=rsem,
            device_id=at(0, xh, 1 - c), device_id_type=MESH).wait_recv()

    count = [0]

    def z_push(d, step):
        here = block(-d, xh, c)
        push(here, here, z_send.at[count[0]], z_recv.at[(d + step) % NZ], at(step, xh, c))
        count[0] += 1

    def share(d):
        here = block(-d, xh, c)
        push(here, here, x_send.at[d % NZ], x_recv.at[d % NZ], at(0, 1 - xh, c))
        push(here, here, c_send.at[d % NZ], c_recv.at[d % NZ], at(0, xh, 1 - c))

    def share_x(ds):
        for d in ds:
            here = block(-d, 1 - xh, c)
            landed(here, x_recv.at[d % NZ])
            push(here, here, d_send.at[d % NZ], d_recv.at[d % NZ], at(0, xh, 1 - c))

    for step in (3, -3, 1, -1):
        z_push(0, step)
    share(0)

    loads[1].wait()
    for i in range(rows // LANES):
        sums = jnp.zeros((LANES, LANES), jnp.float32)
        for j in range(cols // LANES):
            v = g[i * LANES:(i + 1) * LANES, j * LANES:(j + 1) * LANES].astype(jnp.float32)
            sums = sums + v * v
        sq_mine[:, i * LANES:(i + 1) * LANES] = jnp.sum(jnp.transpose(sums), axis=0, keepdims=True)
    for k in range(1, NY):
        push(sq_mine, sq_got.at[k - 1], s_send.at[k - 1], s_recv.at[k - 1], y_peer(k))

    for d in FIRST:
        landed(block(-d, xh, c), z_recv.at[d % NZ])
        if d == 3:
            for step in (3, 1, -1):
                z_push(d, step)
        if d == -3:
            for step in (-3, -1, 1):
                z_push(d, step)
        share(d)
    share_x((0,))
    for d in SECOND:
        landed(block(-d, xh, c), z_recv.at[d % NZ])
        z_push(d, 1)
        z_push(d, -1)
        if d == -6:
            turn = 1 - 2 * c
            here = block(-6 * turn, xh, c)
            push(here, here, z_send.at[count[0]], z_recv.at[8], at(2 * turn, xh, c))
            count[0] += 1
        share(d)
    share_x(FIRST[:2])
    for d in THIRD:
        landed(block(-d, xh, c), z_recv.at[d % NZ])
        share(d)

    total = sq_mine[...]
    for k in range(1, NY):
        landed(sq_got.at[k - 1], s_recv.at[k - 1])
        total = total + sq_got[k - 1]
    sq_pair[...] = total
    push(sq_pair, sq_far, s_send.at[NY - 1], s_recv.at[NY - 1], x_peer)
    share_x(FIRST[2:])

    for d in LAST:
        landed(block(-d, xh, c), z_recv.at[d % NZ])
        share(d)
    share_x(SECOND)
    for d in (0,) + FIRST + SECOND + THIRD + LAST:
        landed(block(-d, xh, 1 - c), c_recv.at[d % NZ])

    def product(xh_of, i):
        first = pl.multiple_of(xh_of * half, half)
        return lax.dot_general(
            qall[pl.ds(first, half), :], g[i * size:(i + 1) * size, :],
            (((1,), (1,)), ((), ())), preferred_element_type=jnp.float32)

    def multiply_a(i):
        value = product(xh, i)
        for b in range(NF):
            pa[i, b] = value[b * per:(b + 1) * per].astype(jnp.bfloat16)
        for k in (2, 1, 3):
            to = lax.rem(y + k, NY)
            push(pa.at[i, pl.ds(to * 2, 2)], a_got.at[i, k - 1],
                 ay_send.at[i, k - 1], ay_recv.at[i, k - 1], y_peer(k))

    def multiply_b(i):
        value = product(1 - xh, i)
        for b in range(NF):
            pb[i, b % 2, b // 2] = value[b * per:(b + 1) * per].astype(jnp.bfloat16)
        push(pb.at[i, 1 - xl], bx_got.at[i], bx_send.at[i], bx_recv.at[i], x_peer)

    def relay_a(i):
        near = pa[i, y * 2 + xl].astype(jnp.float32)
        far = pa[i, y * 2 + 1 - xl].astype(jnp.float32)
        for k in range(1, NY):
            landed(a_got.at[i, k - 1], ay_recv.at[i, k - 1])
            near = near + a_got[i, k - 1, xl].astype(jnp.float32)
            far = far + a_got[i, k - 1, 1 - xl].astype(jnp.float32)
        a_own[i] = near
        a_out[i] = far.astype(jnp.bfloat16)
        push(a_out.at[i], ax_got.at[i], ax_send.at[i], ax_recv.at[i], x_peer)

    def relay_b(i):
        landed(bx_got.at[i], bx_recv.at[i])
        for k in (2, 1, 3, 0):
            to = lax.rem(y + k, NY)
            both = pb[i, xl, to].astype(jnp.float32) + bx_got[i, to].astype(jnp.float32)
            if k == 0:
                b_own[i] = both
            else:
                b_out[i, k - 1] = both.astype(jnp.bfloat16)
                push(b_out.at[i, k - 1], by_got.at[i, k - 1],
                     by_send.at[i, k - 1], by_recv.at[i, k - 1], y_peer(k))

    for i, ds in enumerate((THIRD, LAST[:2], LAST[2:], ())):
        multiply_a(i)
        share_x(ds)
    for d in (0,) + FIRST + SECOND + THIRD + LAST:
        landed(block(-d, 1 - xh, 1 - c), d_recv.at[d % NZ])
    multiply_b(0)
    multiply_b(1)
    relay_a(0)
    multiply_b(2)
    multiply_b(3)

    landed(sq_far, s_recv.at[NY - 1])
    loads[2].wait()
    factor[...] = lw[...] / jnp.sqrt((sq_pair[...] + sq_far[...]) / (cols * NF) + NORM_EPS)

    relay_a(1)
    relay_b(0)
    relay_a(2)
    relay_b(1)
    relay_a(3)
    relay_b(2)
    relay_b(3)

    column_sum = jnp.zeros((1, LANES), jnp.float32)
    group = per // 2
    for i in range(CHUNKS):
        scale = factor[:, i * size:(i + 1) * size]
        landed(ax_got.at[i], ax_recv.at[i])
        own = (a_own[i] + ax_got[i].astype(jnp.float32)) * scale
        other = b_own[i]
        for k in range(1, NY):
            landed(by_got.at[i, k - 1], by_recv.at[i, k - 1])
            other = other + by_got[i, k - 1].astype(jnp.float32)
        other = other * scale
        low, high = jnp.where(xh == 0, own, other), jnp.where(xh == 0, other, own)
        value = jnp.transpose(jnp.concatenate(
            [low[:group], high[:group], low[group:], high[group:]], axis=0))
        scored[i * size:(i + 1) * size, :] = value
        column_sum = column_sum + jnp.sum(value, axis=0, keepdims=True)
    own_mean = column_sum / rows
    off = scored[...] - own_mean
    stat_mine[0:1, :] = own_mean
    stat_mine[1:2, :] = jnp.sum(off * off, axis=0, keepdims=True)

    def stat_copy(i):
        return pltpu.make_async_remote_copy(
            src_ref=stat_mine, dst_ref=stat_got.at[i - 1],
            send_sem=t_send.at[i - 1], recv_sem=t_recv.at[i - 1],
            device_id=(lax.rem(r + i, NR), f), device_id_type=MESH)

    far_first = sorted(range(1, NR), key=lambda i: abs(i - NR // 2))
    for i in far_first:
        stat_copy(i).start()

    @pl.loop(1, NR)
    def _(i):
        stat_copy(i).wait_recv()

    means = stat_got[:, 0, :]
    mean = (jnp.sum(means, axis=0, keepdims=True) + own_mean) / NR
    apart = means - mean
    own_apart = own_mean - mean
    spread = jnp.sum(stat_got[:, 1, :], axis=0, keepdims=True) + stat_mine[1:2, :]
    spread = spread + rows * (jnp.sum(apart * apart, axis=0, keepdims=True) + own_apart * own_apart)
    scale = lax.rsqrt(spread / (rows * NR) + VAR_EPS)
    o_ref[...] = ((scored[...] - mean) * scale).astype(o_ref.dtype)

    for copy in sends:
        copy.wait_send()

    @pl.loop(1, NR)
    def _(i):
        stat_copy(i).wait_send()


def body(gradients, queries, loss_weight):
    rows, cols = gradients.shape
    width = queries.shape[0] * NR // NF
    per, size = width // 2, rows // CHUNKS
    half, f32 = jnp.bfloat16, jnp.float32
    vmem, dma = pltpu.VMEM, pltpu.SemaphoreType.DMA
    return pl.pallas_call(
        kernel,
        out_shape=jax.ShapeDtypeStruct((rows, width), jnp.bfloat16),
        in_specs=[pl.BlockSpec(memory_space=pltpu.HBM)] * 3,
        out_specs=pl.BlockSpec(memory_space=pltpu.VMEM),
        scratch_shapes=[
            vmem((rows, cols), half),
            vmem((NR * QB, cols), half),
            vmem((1, rows), f32),
            vmem((CHUNKS, NF, per, size), half),
            vmem((CHUNKS, 2, NY, per, size), half),
            vmem((CHUNKS, NY - 1, 2, per, size), half),
            vmem((CHUNKS, per, size), half),
            vmem((CHUNKS, per, size), f32),
            vmem((CHUNKS, per, size), half),
            vmem((CHUNKS, NY, per, size), half),
            vmem((CHUNKS, NY - 1, per, size), half),
            vmem((CHUNKS, per, size), f32),
            vmem((CHUNKS, NY - 1, per, size), half),
            vmem((1, rows), f32),
            vmem((NY - 1, 1, rows), f32),
            vmem((1, rows), f32),
            vmem((1, rows), f32),
            vmem((1, rows), f32),
            vmem((rows, width), f32),
            vmem((2, width), f32),
            vmem((NR - 1, 2, width), f32),
            dma((3,)),
            dma((NZ - 1,)), dma((NZ,)), dma((NZ,)), dma((NZ,)),
            dma((NZ,)), dma((NZ,)), dma((NZ,)), dma((NZ,)),
            dma((CHUNKS, NY - 1)), dma((CHUNKS, NY - 1)), dma((CHUNKS,)), dma((CHUNKS,)),
            dma((CHUNKS,)), dma((CHUNKS,)), dma((CHUNKS, NY - 1)), dma((CHUNKS, NY - 1)),
            dma((NY,)), dma((NY,)), dma((NR - 1,)), dma((NR - 1,)),
        ],
        compiler_params=pltpu.CompilerParams(
            collective_id=0, has_side_effects=True, vmem_limit_bytes=60 * 2**20),
        cost_estimate=pl.CostEstimate(
            flops=2 * rows * NR * QB * cols, bytes_accessed=2 * rows * (cols + width), transcendentals=0),
        name="scores",
    )(gradients, queries, loss_weight.reshape(1, rows))


def solution(mesh):
    in_specs = (P("rows", "feat"), P("rows", "feat"), P("rows"))
    out_specs = P("rows", "feat")
    return jax.shard_map(body, mesh=mesh, in_specs=in_specs, out_specs=out_specs, check_vma=False)
```

```python
import math
import jax
import jax.numpy as jnp
from jax import lax
from jax.experimental import pallas as pl
from jax.experimental.pallas import tpu as pltpu
from jax.sharding import PartitionSpec as P

NORM_EPS = 1e-06
VAR_EPS = 1e-05

NZ, NR, NF, NY = 16, 64, 8, 4
QB = 16
CHUNKS = 8
LANES = 128
KINDS = "YYYYYxxx"
MESH = pl.DeviceIdType.MESH
EARLY = (0, 1)
SCHEDULE = [(3, 0), (2, 4), (3, 1), (2, 5), (3, 2), (2, 6), (3, 3), (2, 7), (3, 4), (3, 5), (3, 6), (3, 7)]
SCHEDULE += [(4, i) for i in range(CHUNKS)]


FIRST, SECOND = (3, -3, 1, -1), (6, -6)
THIRD, LAST = (4, -4, 2, -2), (7, -7, 5, -5, 8)


def kernel(
    g_hbm, q_hbm, lw_hbm, o_hbm,
    o_ref, g, qall, lw, part, y_got, y_out, own, x_out, x_got,
    sq_mine, sq_got, sq_pair, sq_far, factor, turned, scored, stat_mine, stat_got,
    l_sem, o_sem, z_recv, x_recv, c_recv, y_recv, p_recv, s_recv, t_recv,
):
    r, f = lax.axis_index("rows"), lax.axis_index("feat")
    z, xh, c = r // 4, lax.rem(r // 2, 2), lax.rem(r, 2)
    y, xl = f // 2, lax.rem(f, 2)
    rows, cols = g.shape
    size = rows // 2
    portion = qall.shape[0] // 4
    per = portion // NF

    def at(dz, xh_to, c_to):
        return (lax.rem(z + dz + NZ, NZ) * 4 + xh_to * 2 + c_to, f)

    def y_peer(k):
        return (r, lax.rem(y + k, NY) * 2 + xl)

    x_peer = (r, y * 2 + 1 - xl)

    def block(dz, xh_of, c_of):
        first = (xh_of * 2 + c_of) * portion + lax.rem(z + dz + NZ, NZ) * QB
        return qall.at[pl.ds(pl.multiple_of(first, QB), QB)]

    def whole(xh_of, c_of):
        first = (xh_of * 2 + c_of) * portion
        return qall.at[pl.ds(pl.multiple_of(first, portion), portion)]

    loads = [
        pltpu.make_async_copy(q_hbm, block(0, xh, c), l_sem.at[0]),
        pltpu.make_async_copy(g_hbm, g, l_sem.at[1]),
        pltpu.make_async_copy(lw_hbm, lw, l_sem.at[2]),
    ]
    for load in loads:
        load.start()

    barrier = pltpu.get_barrier_semaphore()
    greet = [at(d, xh, c) for d in (3, -3, 4 * c - 2, 1, -1)]
    greet += [at(0, 1 - xh, c), at(0, xh, 1 - c), x_peer]
    greet += [y_peer(k) for k in range(1, NY)]
    for device in greet:
        pl.semaphore_signal(barrier, inc=1, device_id=device, device_id_type=MESH)
    loads[0].wait()
    pl.semaphore_wait(barrier, len(greet))

    sent = [0, 0, 0]

    def push(src, dst, group, rsem, device):
        pltpu.make_async_remote_copy(
            src_ref=src, dst_ref=dst, send_sem=o_sem.at[group], recv_sem=rsem,
            device_id=device, device_id_type=MESH).start()
        if group < 3:
            sent[group] += math.prod(src.shape) // cols

    def waiter(ref, ssem, rsem):
        return pltpu.make_async_remote_copy(
            src_ref=ref, dst_ref=ref, send_sem=ssem, recv_sem=rsem,
            device_id=at(0, xh, 1 - c), device_id_type=MESH)

    def landed(dst, rsem):
        waiter(dst, o_sem.at[0], rsem).wait_recv()

    def z_push(d, step):
        here = block(-d, xh, c)
        push(here, here, 0, z_recv.at[(d + step) % NZ], at(step, xh, c))

    def share(d):
        here = block(-d, xh, c)
        push(here, here, 0, x_recv.at[d % NZ], at(0, 1 - xh, c))
        push(here, here, 0, c_recv.at[0], at(0, xh, 1 - c))

    def share_x(ds):
        for d in ds:
            here = block(-d, 1 - xh, c)
            landed(here, x_recv.at[d % NZ])
            push(here, here, 0, c_recv.at[1], at(0, xh, 1 - c))

    for step in (3, -3):
        z_push(0, step)
    share(0)

    loads[1].wait()
    for i in range(rows // LANES):
        sums = jnp.zeros((LANES, LANES), jnp.float32)
        for j in range(cols // LANES):
            v = g[i * LANES:(i + 1) * LANES, j * LANES:(j + 1) * LANES].astype(jnp.float32)
            sums = sums + v * v
        sq_mine[:, i * LANES:(i + 1) * LANES] = jnp.sum(jnp.transpose(sums), axis=0, keepdims=True)
    for k in range(1, NY):
        push(sq_mine, sq_got.at[k - 1], 3, s_recv.at[0], y_peer(k))

    for d in FIRST:
        landed(block(-d, xh, c), z_recv.at[d % NZ])
        if abs(d) == 3:
            z_push(d, d)
        if d == -3:
            for step in (1, -1):
                z_push(0, step)
            for near in (3, -3):
                for step in (1, -1):
                    z_push(near, step)
            share(3)
        if d != 3:
            share(d)
    share_x((0,))
    for d in SECOND:
        landed(block(-d, xh, c), z_recv.at[d % NZ])
        z_push(d, 1)
        z_push(d, -1)
        if d == -6:
            turn = 1 - 2 * c
            here = block(-6 * turn, xh, c)
            push(here, here, 0, z_recv.at[8], at(2 * turn, xh, c))
        share(d)
    share_x(FIRST[:2])
    for d in THIRD:
        landed(block(-d, xh, c), z_recv.at[d % NZ])
        share(d)

    total = sq_mine[...]
    landed(sq_got, s_recv.at[0])
    for k in range(1, NY):
        total = total + sq_got[k - 1]
    sq_pair[...] = total
    push(sq_pair, sq_far, 4, s_recv.at[1], x_peer)
    share_x(FIRST[2:])

    for d in LAST:
        landed(block(-d, xh, c), z_recv.at[d % NZ])
        share(d)
    def y_row(k):
        return lax.rem(y + k + NY, NY)

    def source(i):
        return (xh if i < 4 else 1 - xh), (c if i % 4 < 2 else 1 - c)

    def span(i):
        return slice(i % 2 * size, (i % 2 + 1) * size)

    def y_push(i, src, slot, wide, k):
        dst = y_got.at[i, slot] if wide else y_got.at[i, slot, 0]
        alone = slot == 1 and KINDS[i] in "YX"
        push(src, dst, 1, y_recv.at[i, int(alone)], y_peer(k % NY))

    def y_wait(i, alone=False):
        if alone:
            ref = y_got.at[i, 1]
        else:
            ref = y_got.at[i, 0:2] if KINDS[i] in "YX" else y_got.at[i]
        if KINDS[i] in "Xx":
            ref = ref.at[0] if alone else ref.at[:, 0]
        landed(ref, y_recv.at[i, int(alone)])

    def sign(i):
        return 1 if i % 2 == 0 else -1

    def wide_part(i, k):
        return part.at[i, pl.ds(y_row(k) * 2, 2)]

    def multiply(i):
        value = lax.dot_general(
            whole(*source(i))[...], g[span(i), :],
            (((1,), (1,)), ((), ())), preferred_element_type=jnp.float32)
        y_first = KINDS[i] in "Yy"
        for b in range(NF):
            part[i, b if y_first else b % 2 * NY + b // 2] = value[b * per:(b + 1) * per].astype(jnp.bfloat16)
        s = sign(i)
        if KINDS[i] == "Y":
            y_push(i, wide_part(i, 2), 1, True, s)
            y_push(i, wide_part(i, -s), 0, True, -s)
        elif KINDS[i] == "y":
            for k in (2, 1, 3):
                y_push(i, wide_part(i, k), k - 1, True, k)
        else:
            push(part.at[i, pl.ds((1 - xl) * NY, NY)], x_got.at[i], 2, p_recv.at[i], x_peer)

    def second(i):
        s = sign(i)
        if KINDS[i] == "Y":
            y_wait(i, True)
            both = wide_part(i, s)[...].astype(jnp.float32) + y_got[i, 1].astype(jnp.float32)
            y_out[i, 0:2] = both.astype(jnp.bfloat16)
            y_push(i, y_out.at[i, 0:2], 2, True, s)
        elif KINDS[i] in "Xx":
            landed(x_got.at[i], p_recv.at[i])
            for k in (2, 1, 3, 0):
                to = y_row(k)
                both = part[i, xl * NY + to].astype(jnp.float32) + x_got[i, to].astype(jnp.float32)
                if k == 0:
                    own[i] = both
                    continue
                y_out[i, k - 1] = both.astype(jnp.bfloat16)
                if KINDS[i] == "x":
                    y_push(i, y_out.at[i, k - 1], k - 1, False, k)
                elif k == 2:
                    y_push(i, y_out.at[i, 1], 1, False, s)
                elif k == -s % NY:
                    y_push(i, y_out.at[i, k - 1], 0, False, -s)

    def third(i):
        s = sign(i)
        if KINDS[i] in "Yy":
            near = part[i, y * 2 + xl].astype(jnp.float32)
            far = part[i, y * 2 + 1 - xl].astype(jnp.float32)
            y_wait(i)
            for slot in (0, 2) if KINDS[i] == "Y" else (0, 1, 2):
                near = near + y_got[i, slot, xl].astype(jnp.float32)
                far = far + y_got[i, slot, 1 - xl].astype(jnp.float32)
            own[i] = near
            x_out[i] = far.astype(jnp.bfloat16)
            push(x_out.at[i], x_got.at[i, 0], 2, p_recv.at[i], x_peer)
        elif KINDS[i] == "X":
            y_wait(i, True)
            mine = s % NY - 1
            both = y_out[i, mine].astype(jnp.float32) + y_got[i, 1, 0].astype(jnp.float32)
            y_out[i, 3] = both.astype(jnp.bfloat16)
            y_push(i, y_out.at[i, 3], 2, False, s)

    def finish(i):
        raw = own[i]
        if KINDS[i] in "Yy":
            landed(x_got.at[i, 0], p_recv.at[i])
            raw = raw + x_got[i, 0].astype(jnp.float32)
        else:
            y_wait(i)
            for slot in (0, 2) if KINDS[i] == "X" else (0, 1, 2):
                raw = raw + y_got[i, slot, 0].astype(jnp.float32)
        raw = raw * factor[:, span(i)]
        xh_of, c_of = source(i)
        for low in range(per // QB):
            first = low * (4 * QB) + (xh_of * 2 + c_of) * QB
            turned[pl.ds(pl.multiple_of(first, QB), QB), span(i)] = raw[low * QB:(low + 1) * QB]

    def turn(h):
        value = jnp.transpose(turned[:, h * size:(h + 1) * size])
        scored[h * size:(h + 1) * size, :] = value
        return jnp.sum(value, axis=0, keepdims=True)

    multiply(0)
    multiply(1)
    share_x(SECOND)
    landed(whole(xh, 1 - c), c_recv.at[0])
    multiply(2)
    multiply(3)
    share_x(THIRD)
    share_x(LAST)
    multiply(4)
    multiply(5)
    for i in EARLY:
        second(i)
    landed(whole(1 - xh, 1 - c), c_recv.at[1])
    multiply(6)
    multiply(7)
    landed(sq_far, s_recv.at[1])
    loads[2].wait()
    factor[...] = lw[...] / jnp.sqrt((sq_pair[...] + sq_far[...]) / (cols * NF) + NORM_EPS)
    for i in range(4):
        if i not in EARLY:
            second(i)
    for step, i in SCHEDULE:
        (second, third, finish)[step - 2](i)
    column_sum = turn(0) + turn(1)
    own_mean = column_sum / rows
    off = scored[...] - own_mean
    stat_mine[0:1, :] = own_mean
    stat_mine[1:2, :] = jnp.sum(off * off, axis=0, keepdims=True)

    for i in sorted(range(1, NR), key=lambda i: abs(i - NR // 2)):
        push(stat_mine, stat_got.at[i - 1], 5, t_recv, (lax.rem(r + i, NR), f))
    for group, count in enumerate(sent):
        waiter(qall.at[pl.ds(0, count)], o_sem.at[group], t_recv).wait_send()
    waiter(sq_got, o_sem.at[3], t_recv).wait_send()
    waiter(sq_far, o_sem.at[4], t_recv).wait_send()
    stat_wait = waiter(stat_got, o_sem.at[5], t_recv)
    stat_wait.wait_recv()

    means = stat_got[:, 0, :]
    mean = (jnp.sum(means, axis=0, keepdims=True) + own_mean) / NR
    apart = means - mean
    own_apart = own_mean - mean
    spread = jnp.sum(stat_got[:, 1, :], axis=0, keepdims=True) + stat_mine[1:2, :]
    spread = spread + rows * (jnp.sum(apart * apart, axis=0, keepdims=True) + own_apart * own_apart)
    scale = lax.rsqrt(spread / (rows * NR) + VAR_EPS)
    o_ref[...] = ((scored[...] - mean) * scale).astype(o_ref.dtype)
    final = pltpu.make_async_copy(o_ref, o_hbm, l_sem.at[3])
    final.start()
    stat_wait.wait_send()
    final.wait()


def body(gradients, queries, loss_weight):
    rows, cols = gradients.shape
    width = queries.shape[0] * NR // NF
    per, size = width // 4, rows // 2
    half, f32 = jnp.bfloat16, jnp.float32
    vmem, dma = pltpu.VMEM, pltpu.SemaphoreType.DMA
    return pl.pallas_call(
        kernel,
        out_shape=jax.ShapeDtypeStruct((rows, width), jnp.bfloat16),
        in_specs=[pl.BlockSpec(memory_space=pltpu.HBM)] * 3,
        out_specs=pl.BlockSpec(memory_space=pltpu.HBM),
        scratch_shapes=[
            vmem((rows, width), half),
            vmem((rows, cols), half),
            vmem((NR * QB, cols), half),
            vmem((1, rows), f32),
            vmem((CHUNKS, NF, per, size), half),
            vmem((CHUNKS, NY - 1, 2, per, size), half),
            vmem((CHUNKS, NY, per, size), half),
            vmem((CHUNKS, per, size), f32),
            vmem((CHUNKS, per, size), half),
            vmem((CHUNKS, NY, per, size), half),
            vmem((1, rows), f32),
            vmem((NY - 1, 1, rows), f32),
            vmem((1, rows), f32),
            vmem((1, rows), f32),
            vmem((1, rows), f32),
            vmem((width, rows), f32),
            vmem((rows, width), f32),
            vmem((2, width), f32),
            vmem((NR - 1, 2, width), f32),
            dma((4,)), dma((6,)), dma((NZ,)), dma((NZ,)), dma((2,)),
            dma((CHUNKS, 2)), dma((CHUNKS,)), dma((2,)), dma,
        ],
        compiler_params=pltpu.CompilerParams(
            collective_id=0, has_side_effects=True, vmem_limit_bytes=60 * 2**20),
        cost_estimate=pl.CostEstimate(
            flops=2 * rows * NR * QB * cols, bytes_accessed=2 * rows * (cols + width), transcendentals=0),
        name="scores",
    )(gradients, queries, loss_weight.reshape(1, rows))


def solution(mesh):
    in_specs = (P("rows", "feat"), P("rows", "feat"), P("rows"))
    out_specs = P("rows", "feat")
    return jax.shard_map(body, mesh=mesh, in_specs=in_specs, out_specs=out_specs, check_vma=False)
```

```python
import math
import jax
import jax.numpy as jnp
from jax import lax
from jax.experimental import pallas as pl
from jax.experimental.pallas import tpu as pltpu
from jax.sharding import PartitionSpec as P

NORM_EPS = 1e-06
VAR_EPS = 1e-05

NZ, NR, NF, NY = 16, 64, 8, 4
QB = 16
CHUNKS = 8
LANES = 128
KINDS = "YYYYYxxx"
MESH = pl.DeviceIdType.MESH
EARLY = (0, 1)
SCHEDULE = [(3, 0), (2, 4), (3, 1), (2, 5), (3, 2), (2, 6), (3, 3), (2, 7), (3, 4), (3, 5), (3, 6), (3, 7)]
SCHEDULE += [(4, i) for i in range(CHUNKS)]


FIRST, SECOND = (3, -3, 1, -1), (6, -6)
THIRD, LAST = (4, -4, 2, -2), (7, -7, 5, -5, 8)


def kernel(
    g_hbm, q_hbm, lw_hbm, o_ref,
    g, qall, lw, part, y_got, y_out, own, x_out, x_got,
    sq_mine, sq_got, sq_pair, sq_far, factor, turned, scored, stat_mine, stat_got,
    l_sem, o_sem, z_recv, x_recv, c_recv, y_recv, p_recv, s_recv, t_recv,
):
    r, f = lax.axis_index("rows"), lax.axis_index("feat")
    z, xh, c = r // 4, lax.rem(r // 2, 2), lax.rem(r, 2)
    y, xl = f // 2, lax.rem(f, 2)
    rows, cols = g.shape
    size = rows // 2
    portion = qall.shape[0] // 4
    per = portion // NF

    def at(dz, xh_to, c_to):
        return (lax.rem(z + dz + NZ, NZ) * 4 + xh_to * 2 + c_to, f)

    def y_peer(k):
        return (r, lax.rem(y + k, NY) * 2 + xl)

    x_peer = (r, y * 2 + 1 - xl)

    def block(dz, xh_of, c_of):
        first = (xh_of * 2 + c_of) * portion + lax.rem(z + dz + NZ, NZ) * QB
        return qall.at[pl.ds(pl.multiple_of(first, QB), QB)]

    def whole(xh_of, c_of):
        first = (xh_of * 2 + c_of) * portion
        return qall.at[pl.ds(pl.multiple_of(first, portion), portion)]

    loads = [
        pltpu.make_async_copy(q_hbm, block(0, xh, c), l_sem.at[0]),
        pltpu.make_async_copy(g_hbm, g, l_sem.at[1]),
        pltpu.make_async_copy(lw_hbm, lw, l_sem.at[2]),
    ]
    for load in loads:
        load.start()

    barrier = pltpu.get_barrier_semaphore()
    greet = [at(d, xh, c) for d in (3, -3, 4 * c - 2, 1, -1)]
    greet += [at(0, 1 - xh, c), at(0, xh, 1 - c), x_peer]
    greet += [y_peer(k) for k in range(1, NY)]
    for device in greet:
        pl.semaphore_signal(barrier, inc=1, device_id=device, device_id_type=MESH)
    loads[0].wait()
    pl.semaphore_wait(barrier, len(greet))

    sent = [0, 0, 0]

    def push(src, dst, group, rsem, device):
        pltpu.make_async_remote_copy(
            src_ref=src, dst_ref=dst, send_sem=o_sem.at[group], recv_sem=rsem,
            device_id=device, device_id_type=MESH).start()
        if group < 3:
            sent[group] += math.prod(src.shape) // cols

    def waiter(ref, ssem, rsem):
        return pltpu.make_async_remote_copy(
            src_ref=ref, dst_ref=ref, send_sem=ssem, recv_sem=rsem,
            device_id=at(0, xh, 1 - c), device_id_type=MESH)

    def landed(dst, rsem):
        waiter(dst, o_sem.at[0], rsem).wait_recv()

    def z_push(d, step):
        here = block(-d, xh, c)
        push(here, here, 0, z_recv.at[(d + step) % NZ], at(step, xh, c))

    def share(d):
        here = block(-d, xh, c)
        push(here, here, 0, x_recv.at[d % NZ], at(0, 1 - xh, c))
        push(here, here, 0, c_recv.at[0], at(0, xh, 1 - c))

    def share_x(ds):
        for d in ds:
            here = block(-d, 1 - xh, c)
            landed(here, x_recv.at[d % NZ])
            push(here, here, 0, c_recv.at[1], at(0, xh, 1 - c))

    for step in (3, -3, 1, -1):
        z_push(0, step)
    share(0)

    loads[1].wait()
    for i in range(rows // LANES):
        sums = jnp.zeros((LANES, LANES), jnp.float32)
        for j in range(cols // LANES):
            v = g[i * LANES:(i + 1) * LANES, j * LANES:(j + 1) * LANES].astype(jnp.float32)
            sums = sums + v * v
        sq_mine[:, i * LANES:(i + 1) * LANES] = jnp.sum(jnp.transpose(sums), axis=0, keepdims=True)
    for k in range(1, NY):
        push(sq_mine, sq_got.at[k - 1], 3, s_recv.at[0], y_peer(k))

    for d in FIRST:
        landed(block(-d, xh, c), z_recv.at[d % NZ])
        if abs(d) == 3:
            z_push(d, d)
            if d == -3:
                for near in (3, -3):
                    for step in (1, -1):
                        z_push(near, step)
        share(d)
    share_x((0,))
    for d in SECOND:
        landed(block(-d, xh, c), z_recv.at[d % NZ])
        z_push(d, 1)
        z_push(d, -1)
        if d == -6:
            turn = 1 - 2 * c
            here = block(-6 * turn, xh, c)
            push(here, here, 0, z_recv.at[8], at(2 * turn, xh, c))
        share(d)
    share_x(FIRST[:2])
    for d in THIRD:
        landed(block(-d, xh, c), z_recv.at[d % NZ])
        share(d)

    total = sq_mine[...]
    landed(sq_got, s_recv.at[0])
    for k in range(1, NY):
        total = total + sq_got[k - 1]
    sq_pair[...] = total
    push(sq_pair, sq_far, 4, s_recv.at[1], x_peer)
    share_x(FIRST[2:])

    for d in LAST:
        landed(block(-d, xh, c), z_recv.at[d % NZ])
        share(d)
    def y_row(k):
        return lax.rem(y + k + NY, NY)

    def source(i):
        return (xh if i < 4 else 1 - xh), (c if i % 4 < 2 else 1 - c)

    def span(i):
        return slice(i % 2 * size, (i % 2 + 1) * size)

    def y_push(i, src, slot, wide, k):
        dst = y_got.at[i, slot] if wide else y_got.at[i, slot, 0]
        alone = slot == 1 and KINDS[i] in "YX"
        push(src, dst, 1, y_recv.at[i, int(alone)], y_peer(k % NY))

    def y_wait(i, alone=False):
        if alone:
            ref = y_got.at[i, 1]
        else:
            ref = y_got.at[i, 0:2] if KINDS[i] in "YX" else y_got.at[i]
        if KINDS[i] in "Xx":
            ref = ref.at[0] if alone else ref.at[:, 0]
        landed(ref, y_recv.at[i, int(alone)])

    def sign(i):
        return 1 if i % 2 == 0 else -1

    def wide_part(i, k):
        return part.at[i, pl.ds(y_row(k) * 2, 2)]

    def multiply(i):
        value = lax.dot_general(
            whole(*source(i))[...], g[span(i), :],
            (((1,), (1,)), ((), ())), preferred_element_type=jnp.float32)
        y_first = KINDS[i] in "Yy"
        for b in range(NF):
            part[i, b if y_first else b % 2 * NY + b // 2] = value[b * per:(b + 1) * per].astype(jnp.bfloat16)
        s = sign(i)
        if KINDS[i] == "Y":
            y_push(i, wide_part(i, 2), 1, True, s)
            y_push(i, wide_part(i, -s), 0, True, -s)
        elif KINDS[i] == "y":
            for k in (2, 1, 3):
                y_push(i, wide_part(i, k), k - 1, True, k)
        else:
            push(part.at[i, pl.ds((1 - xl) * NY, NY)], x_got.at[i], 2, p_recv.at[i], x_peer)

    def second(i):
        s = sign(i)
        if KINDS[i] == "Y":
            y_wait(i, True)
            both = wide_part(i, s)[...].astype(jnp.float32) + y_got[i, 1].astype(jnp.float32)
            y_out[i, 0:2] = both.astype(jnp.bfloat16)
            y_push(i, y_out.at[i, 0:2], 2, True, s)
        elif KINDS[i] in "Xx":
            landed(x_got.at[i], p_recv.at[i])
            for k in (2, 1, 3, 0):
                to = y_row(k)
                both = part[i, xl * NY + to].astype(jnp.float32) + x_got[i, to].astype(jnp.float32)
                if k == 0:
                    own[i] = both
                    continue
                y_out[i, k - 1] = both.astype(jnp.bfloat16)
                if KINDS[i] == "x":
                    y_push(i, y_out.at[i, k - 1], k - 1, False, k)
                elif k == 2:
                    y_push(i, y_out.at[i, 1], 1, False, s)
                elif k == -s % NY:
                    y_push(i, y_out.at[i, k - 1], 0, False, -s)

    def third(i):
        s = sign(i)
        if KINDS[i] in "Yy":
            near = part[i, y * 2 + xl].astype(jnp.float32)
            far = part[i, y * 2 + 1 - xl].astype(jnp.float32)
            y_wait(i)
            for slot in (0, 2) if KINDS[i] == "Y" else (0, 1, 2):
                near = near + y_got[i, slot, xl].astype(jnp.float32)
                far = far + y_got[i, slot, 1 - xl].astype(jnp.float32)
            own[i] = near
            x_out[i] = far.astype(jnp.bfloat16)
            push(x_out.at[i], x_got.at[i, 0], 2, p_recv.at[i], x_peer)
        elif KINDS[i] == "X":
            y_wait(i, True)
            mine = s % NY - 1
            both = y_out[i, mine].astype(jnp.float32) + y_got[i, 1, 0].astype(jnp.float32)
            y_out[i, 3] = both.astype(jnp.bfloat16)
            y_push(i, y_out.at[i, 3], 2, False, s)

    def finish(i):
        raw = own[i]
        if KINDS[i] in "Yy":
            landed(x_got.at[i, 0], p_recv.at[i])
            raw = raw + x_got[i, 0].astype(jnp.float32)
        else:
            y_wait(i)
            for slot in (0, 2) if KINDS[i] == "X" else (0, 1, 2):
                raw = raw + y_got[i, slot, 0].astype(jnp.float32)
        raw = raw * factor[:, span(i)]
        xh_of, c_of = source(i)
        for low in range(per // QB):
            first = low * (4 * QB) + (xh_of * 2 + c_of) * QB
            turned[pl.ds(pl.multiple_of(first, QB), QB), span(i)] = raw[low * QB:(low + 1) * QB]

    def turn(h):
        value = jnp.transpose(turned[:, h * size:(h + 1) * size])
        scored[h * size:(h + 1) * size, :] = value
        return jnp.sum(value, axis=0, keepdims=True)

    multiply(0)
    multiply(1)
    share_x(SECOND)
    landed(whole(xh, 1 - c), c_recv.at[0])
    multiply(2)
    multiply(3)
    share_x(THIRD)
    share_x(LAST)
    multiply(4)
    multiply(5)
    for i in EARLY:
        second(i)
    landed(whole(1 - xh, 1 - c), c_recv.at[1])
    multiply(6)
    multiply(7)
    landed(sq_far, s_recv.at[1])
    loads[2].wait()
    factor[...] = lw[...] / jnp.sqrt((sq_pair[...] + sq_far[...]) / (cols * NF) + NORM_EPS)
    for i in range(4):
        if i not in EARLY:
            second(i)
    for step, i in SCHEDULE:
        (second, third, finish)[step - 2](i)
    column_sum = turn(0) + turn(1)
    own_mean = column_sum / rows
    off = scored[...] - own_mean
    stat_mine[0:1, :] = own_mean
    stat_mine[1:2, :] = jnp.sum(off * off, axis=0, keepdims=True)

    for i in sorted(range(1, NR), key=lambda i: abs(i - NR // 2)):
        push(stat_mine, stat_got.at[i - 1], 5, t_recv, (lax.rem(r + i, NR), f))
    for group, count in enumerate(sent):
        waiter(qall.at[pl.ds(0, count)], o_sem.at[group], t_recv).wait_send()
    waiter(sq_got, o_sem.at[3], t_recv).wait_send()
    waiter(sq_far, o_sem.at[4], t_recv).wait_send()
    stat_wait = waiter(stat_got, o_sem.at[5], t_recv)
    stat_wait.wait_recv()

    means = stat_got[:, 0, :]
    mean = (jnp.sum(means, axis=0, keepdims=True) + own_mean) / NR
    apart = means - mean
    own_apart = own_mean - mean
    spread = jnp.sum(stat_got[:, 1, :], axis=0, keepdims=True) + stat_mine[1:2, :]
    spread = spread + rows * (jnp.sum(apart * apart, axis=0, keepdims=True) + own_apart * own_apart)
    scale = lax.rsqrt(spread / (rows * NR) + VAR_EPS)
    o_ref[...] = ((scored[...] - mean) * scale).astype(o_ref.dtype)
    stat_wait.wait_send()


def body(gradients, queries, loss_weight):
    rows, cols = gradients.shape
    width = queries.shape[0] * NR // NF
    per, size = width // 4, rows // 2
    half, f32 = jnp.bfloat16, jnp.float32
    vmem, dma = pltpu.VMEM, pltpu.SemaphoreType.DMA
    return pl.pallas_call(
        kernel,
        out_shape=jax.ShapeDtypeStruct((rows, width), jnp.bfloat16),
        in_specs=[pl.BlockSpec(memory_space=pltpu.HBM)] * 3,
        out_specs=pl.BlockSpec(memory_space=pltpu.VMEM),
        scratch_shapes=[
            vmem((rows, cols), half),
            vmem((NR * QB, cols), half),
            vmem((1, rows), f32),
            vmem((CHUNKS, NF, per, size), half),
            vmem((CHUNKS, NY - 1, 2, per, size), half),
            vmem((CHUNKS, NY, per, size), half),
            vmem((CHUNKS, per, size), f32),
            vmem((CHUNKS, per, size), half),
            vmem((CHUNKS, NY, per, size), half),
            vmem((1, rows), f32),
            vmem((NY - 1, 1, rows), f32),
            vmem((1, rows), f32),
            vmem((1, rows), f32),
            vmem((1, rows), f32),
            vmem((width, rows), f32),
            vmem((rows, width), f32),
            vmem((2, width), f32),
            vmem((NR - 1, 2, width), f32),
            dma((3,)), dma((6,)), dma((NZ,)), dma((NZ,)), dma((2,)),
            dma((CHUNKS, 2)), dma((CHUNKS,)), dma((2,)), dma,
        ],
        compiler_params=pltpu.CompilerParams(
            collective_id=0, has_side_effects=True, vmem_limit_bytes=48 * 2**20),
        cost_estimate=pl.CostEstimate(
            flops=2 * rows * NR * QB * cols, bytes_accessed=2 * rows * (cols + width), transcendentals=0),
        name="scores",
    )(*(pltpu.with_memory_space_constraint(v, pltpu.HBM) for v in (gradients, queries, loss_weight.reshape(1, rows))))


def solution(mesh):
    in_specs = (P("rows", "feat"), P("rows", "feat"), P("rows"))
    out_specs = P("rows", "feat")
    return jax.shard_map(body, mesh=mesh, in_specs=in_specs, out_specs=out_specs, check_vma=False)
```

```python
import math
import jax
import jax.numpy as jnp
from jax import lax
from jax.experimental import pallas as pl
from jax.experimental.pallas import tpu as pltpu
from jax.sharding import PartitionSpec as P

NORM_EPS = 1e-06
VAR_EPS = 1e-05

NZ, NR, NF, NY = 16, 64, 8, 4
QB = 16
CHUNKS = 8
LANES = 128
KINDS = "YYYYYxxx"
MESH = pl.DeviceIdType.MESH
EARLY = (0, 1)
SCHEDULE = [(3, 0), (2, 4), (3, 1), (2, 5), (3, 2), (2, 6), (3, 3), (2, 7), (3, 4), (3, 5), (3, 6), (3, 7)]
SCHEDULE += [(4, i) for i in range(CHUNKS)]


FIRST, SECOND = (3, -3, 1, -1), (6, -6)
THIRD, LAST = (4, -4, 2, -2), (7, -7, 5, -5, 8)


def kernel(
    g_hbm, q_hbm, lw_hbm, o_ref,
    g, qall, lw, part, y_got, y_out, own, x_out, x_got,
    sq_mine, sq_got, sq_pair, sq_far, factor, turned, scored, stat_mine, stat_got,
    l_sem, o_sem, z_recv, x_recv, c_recv, y_recv, p_recv, s_recv, t_recv,
):
    r, f = lax.axis_index("rows"), lax.axis_index("feat")
    z, xh, c = r // 4, lax.rem(r // 2, 2), lax.rem(r, 2)
    y, xl = f // 2, lax.rem(f, 2)
    rows, cols = g.shape
    size = rows // 2
    portion = qall.shape[0] // 4
    per = portion // NF

    def at(dz, xh_to, c_to):
        return (lax.rem(z + dz + NZ, NZ) * 4 + xh_to * 2 + c_to, f)

    def y_peer(k):
        return (r, lax.rem(y + k, NY) * 2 + xl)

    x_peer = (r, y * 2 + 1 - xl)

    def block(dz, xh_of, c_of):
        first = (xh_of * 2 + c_of) * portion + lax.rem(z + dz + NZ, NZ) * QB
        return qall.at[pl.ds(pl.multiple_of(first, QB), QB)]

    def whole(xh_of, c_of):
        first = (xh_of * 2 + c_of) * portion
        return qall.at[pl.ds(pl.multiple_of(first, portion), portion)]

    loads = [
        pltpu.make_async_copy(q_hbm, block(0, xh, c), l_sem.at[0]),
        pltpu.make_async_copy(g_hbm, g, l_sem.at[1]),
        pltpu.make_async_copy(lw_hbm, lw, l_sem.at[2]),
    ]
    for load in loads:
        load.start()

    barrier = pltpu.get_barrier_semaphore()
    greet = [at(d, xh, c) for d in (3, -3, 4 * c - 2, 1, -1)]
    greet += [at(0, 1 - xh, c), at(0, xh, 1 - c), x_peer]
    greet += [y_peer(k) for k in range(1, NY)]
    for device in greet:
        pl.semaphore_signal(barrier, inc=1, device_id=device, device_id_type=MESH)
    loads[0].wait()
    pl.semaphore_wait(barrier, len(greet))

    sent = [0, 0, 0]

    def push(src, dst, group, rsem, device):
        pltpu.make_async_remote_copy(
            src_ref=src, dst_ref=dst, send_sem=o_sem.at[group], recv_sem=rsem,
            device_id=device, device_id_type=MESH).start()
        if group < 3:
            sent[group] += math.prod(src.shape) // cols

    def waiter(ref, ssem, rsem):
        return pltpu.make_async_remote_copy(
            src_ref=ref, dst_ref=ref, send_sem=ssem, recv_sem=rsem,
            device_id=at(0, xh, 1 - c), device_id_type=MESH)

    def landed(dst, rsem):
        waiter(dst, o_sem.at[0], rsem).wait_recv()

    def z_push(d, step):
        here = block(-d, xh, c)
        push(here, here, 0, z_recv.at[(d + step) % NZ], at(step, xh, c))

    def share(d):
        here = block(-d, xh, c)
        push(here, here, 0, x_recv.at[d % NZ], at(0, 1 - xh, c))
        push(here, here, 0, c_recv.at[0], at(0, xh, 1 - c))

    def share_x(ds):
        for d in ds:
            here = block(-d, 1 - xh, c)
            landed(here, x_recv.at[d % NZ])
            push(here, here, 0, c_recv.at[1], at(0, xh, 1 - c))

    for step in (3, -3, 1, -1):
        z_push(0, step)
    share(0)

    loads[1].wait()
    for i in range(rows // LANES):
        sums = jnp.zeros((LANES, LANES), jnp.float32)
        for j in range(cols // LANES):
            v = g[i * LANES:(i + 1) * LANES, j * LANES:(j + 1) * LANES].astype(jnp.float32)
            sums = sums + v * v
        sq_mine[:, i * LANES:(i + 1) * LANES] = jnp.sum(jnp.transpose(sums), axis=0, keepdims=True)
    for k in range(1, NY):
        push(sq_mine, sq_got.at[k - 1], 3, s_recv.at[0], y_peer(k))

    for d in FIRST:
        landed(block(-d, xh, c), z_recv.at[d % NZ])
        if abs(d) == 3:
            z_push(d, d)
            if d == -3:
                for near in (3, -3):
                    for step in (1, -1):
                        z_push(near, step)
        share(d)
    share_x((0,))
    for d in SECOND:
        landed(block(-d, xh, c), z_recv.at[d % NZ])
        z_push(d, 1)
        z_push(d, -1)
        if d == -6:
            turn = 1 - 2 * c
            here = block(-6 * turn, xh, c)
            push(here, here, 0, z_recv.at[8], at(2 * turn, xh, c))
        share(d)
    share_x(FIRST[:2])
    for d in THIRD:
        landed(block(-d, xh, c), z_recv.at[d % NZ])
        share(d)

    total = sq_mine[...]
    landed(sq_got, s_recv.at[0])
    for k in range(1, NY):
        total = total + sq_got[k - 1]
    sq_pair[...] = total
    push(sq_pair, sq_far, 4, s_recv.at[1], x_peer)
    share_x(FIRST[2:])

    for d in LAST:
        landed(block(-d, xh, c), z_recv.at[d % NZ])
        share(d)
    def y_row(k):
        return lax.rem(y + k + NY, NY)

    def source(i):
        return (xh if i < 4 else 1 - xh), (c if i % 4 < 2 else 1 - c)

    def span(i):
        return slice(i % 2 * size, (i % 2 + 1) * size)

    def y_push(i, src, slot, wide, k):
        dst = y_got.at[i, slot] if wide else y_got.at[i, slot, 0]
        alone = slot == 1 and KINDS[i] in "YX"
        push(src, dst, 1, y_recv.at[i, int(alone)], y_peer(k % NY))

    def y_wait(i, alone=False):
        if alone:
            ref = y_got.at[i, 1]
        else:
            ref = y_got.at[i, 0:2] if KINDS[i] in "YX" else y_got.at[i]
        if KINDS[i] in "Xx":
            ref = ref.at[0] if alone else ref.at[:, 0]
        landed(ref, y_recv.at[i, int(alone)])

    def sign(i):
        return 1 if i % 2 == 0 else -1

    def wide_part(i, k):
        return part.at[i, pl.ds(y_row(k) * 2, 2)]

    def multiply(i):
        value = lax.dot_general(
            whole(*source(i))[...], g[span(i), :],
            (((1,), (1,)), ((), ())), preferred_element_type=jnp.float32)
        y_first = KINDS[i] in "Yy"
        for b in range(NF):
            part[i, b if y_first else b % 2 * NY + b // 2] = value[b * per:(b + 1) * per].astype(jnp.bfloat16)
        s = sign(i)
        if KINDS[i] == "Y":
            y_push(i, wide_part(i, 2), 1, True, s)
            y_push(i, wide_part(i, -s), 0, True, -s)
        elif KINDS[i] == "y":
            for k in (2, 1, 3):
                y_push(i, wide_part(i, k), k - 1, True, k)
        else:
            push(part.at[i, pl.ds((1 - xl) * NY, NY)], x_got.at[i], 2, p_recv.at[i], x_peer)

    def second(i):
        s = sign(i)
        if KINDS[i] == "Y":
            y_wait(i, True)
            both = wide_part(i, s)[...].astype(jnp.float32) + y_got[i, 1].astype(jnp.float32)
            y_out[i, 0:2] = both.astype(jnp.bfloat16)
            y_push(i, y_out.at[i, 0:2], 2, True, s)
        elif KINDS[i] in "Xx":
            landed(x_got.at[i], p_recv.at[i])
            for k in (2, 1, 3, 0):
                to = y_row(k)
                both = part[i, xl * NY + to].astype(jnp.float32) + x_got[i, to].astype(jnp.float32)
                if k == 0:
                    own[i] = both
                    continue
                y_out[i, k - 1] = both.astype(jnp.bfloat16)
                if KINDS[i] == "x":
                    y_push(i, y_out.at[i, k - 1], k - 1, False, k)
                elif k == 2:
                    y_push(i, y_out.at[i, 1], 1, False, s)
                elif k == -s % NY:
                    y_push(i, y_out.at[i, k - 1], 0, False, -s)

    def third(i):
        s = sign(i)
        if KINDS[i] in "Yy":
            near = part[i, y * 2 + xl].astype(jnp.float32)
            far = part[i, y * 2 + 1 - xl].astype(jnp.float32)
            y_wait(i)
            for slot in (0, 2) if KINDS[i] == "Y" else (0, 1, 2):
                near = near + y_got[i, slot, xl].astype(jnp.float32)
                far = far + y_got[i, slot, 1 - xl].astype(jnp.float32)
            own[i] = near
            x_out[i] = far.astype(jnp.bfloat16)
            push(x_out.at[i], x_got.at[i, 0], 2, p_recv.at[i], x_peer)
        elif KINDS[i] == "X":
            y_wait(i, True)
            mine = s % NY - 1
            both = y_out[i, mine].astype(jnp.float32) + y_got[i, 1, 0].astype(jnp.float32)
            y_out[i, 3] = both.astype(jnp.bfloat16)
            y_push(i, y_out.at[i, 3], 2, False, s)

    def finish(i):
        raw = own[i]
        if KINDS[i] in "Yy":
            landed(x_got.at[i, 0], p_recv.at[i])
            raw = raw + x_got[i, 0].astype(jnp.float32)
        else:
            y_wait(i)
            for slot in (0, 2) if KINDS[i] == "X" else (0, 1, 2):
                raw = raw + y_got[i, slot, 0].astype(jnp.float32)
        raw = raw * factor[:, span(i)]
        xh_of, c_of = source(i)
        for low in range(per // QB):
            first = low * (4 * QB) + (xh_of * 2 + c_of) * QB
            turned[pl.ds(pl.multiple_of(first, QB), QB), span(i)] = raw[low * QB:(low + 1) * QB]

    def turn(h):
        value = jnp.transpose(turned[:, h * size:(h + 1) * size])
        scored[h * size:(h + 1) * size, :] = value
        return jnp.sum(value, axis=0, keepdims=True)

    multiply(0)
    multiply(1)
    share_x(SECOND)
    landed(whole(xh, 1 - c), c_recv.at[0])
    multiply(2)
    multiply(3)
    share_x(THIRD)
    share_x(LAST)
    multiply(5)
    multiply(4)
    for i in EARLY:
        second(i)
    landed(whole(1 - xh, 1 - c), c_recv.at[1])
    multiply(6)
    multiply(7)
    landed(sq_far, s_recv.at[1])
    loads[2].wait()
    factor[...] = lw[...] / jnp.sqrt((sq_pair[...] + sq_far[...]) / (cols * NF) + NORM_EPS)
    for i in range(4):
        if i not in EARLY:
            second(i)
    for step, i in SCHEDULE:
        (second, third, finish)[step - 2](i)
    column_sum = turn(0) + turn(1)
    own_mean = column_sum / rows
    off = scored[...] - own_mean
    stat_mine[0:1, :] = own_mean
    stat_mine[1:2, :] = jnp.sum(off * off, axis=0, keepdims=True)

    for i in sorted(range(1, NR), key=lambda i: abs(i - NR // 2)):
        push(stat_mine, stat_got.at[i - 1], 5, t_recv, (lax.rem(r + i, NR), f))
    for group, count in enumerate(sent):
        waiter(qall.at[pl.ds(0, count)], o_sem.at[group], t_recv).wait_send()
    waiter(sq_got, o_sem.at[3], t_recv).wait_send()
    waiter(sq_far, o_sem.at[4], t_recv).wait_send()
    stat_wait = waiter(stat_got, o_sem.at[5], t_recv)
    stat_wait.wait_recv()

    means = stat_got[:, 0, :]
    mean = (jnp.sum(means, axis=0, keepdims=True) + own_mean) / NR
    apart = means - mean
    own_apart = own_mean - mean
    spread = jnp.sum(stat_got[:, 1, :], axis=0, keepdims=True) + stat_mine[1:2, :]
    spread = spread + rows * (jnp.sum(apart * apart, axis=0, keepdims=True) + own_apart * own_apart)
    scale = lax.rsqrt(spread / (rows * NR) + VAR_EPS)
    o_ref[...] = ((scored[...] - mean) * scale).astype(o_ref.dtype)
    stat_wait.wait_send()


def body(gradients, queries, loss_weight):
    rows, cols = gradients.shape
    width = queries.shape[0] * NR // NF
    per, size = width // 4, rows // 2
    half, f32 = jnp.bfloat16, jnp.float32
    vmem, dma = pltpu.VMEM, pltpu.SemaphoreType.DMA
    return pl.pallas_call(
        kernel,
        out_shape=jax.ShapeDtypeStruct((rows, width), jnp.bfloat16),
        in_specs=[pl.BlockSpec(memory_space=pltpu.HBM)] * 3,
        out_specs=pl.BlockSpec(memory_space=pltpu.VMEM),
        scratch_shapes=[
            vmem((rows, cols), half),
            vmem((NR * QB, cols), half),
            vmem((1, rows), f32),
            vmem((CHUNKS, NF, per, size), half),
            vmem((CHUNKS, NY - 1, 2, per, size), half),
            vmem((CHUNKS, NY, per, size), half),
            vmem((CHUNKS, per, size), f32),
            vmem((CHUNKS, per, size), half),
            vmem((CHUNKS, NY, per, size), half),
            vmem((1, rows), f32),
            vmem((NY - 1, 1, rows), f32),
            vmem((1, rows), f32),
            vmem((1, rows), f32),
            vmem((1, rows), f32),
            vmem((width, rows), f32),
            vmem((rows, width), f32),
            vmem((2, width), f32),
            vmem((NR - 1, 2, width), f32),
            dma((3,)), dma((6,)), dma((NZ,)), dma((NZ,)), dma((2,)),
            dma((CHUNKS, 2)), dma((CHUNKS,)), dma((2,)), dma,
        ],
        compiler_params=pltpu.CompilerParams(
            collective_id=0, has_side_effects=True, vmem_limit_bytes=48 * 2**20),
        cost_estimate=pl.CostEstimate(
            flops=2 * rows * NR * QB * cols, bytes_accessed=2 * rows * (cols + width), transcendentals=0),
        name="scores",
    )(*(pltpu.with_memory_space_constraint(v, pltpu.HBM) for v in (gradients, queries, loss_weight.reshape(1, rows))))


def solution(mesh):
    in_specs = (P("rows", "feat"), P("rows", "feat"), P("rows"))
    out_specs = P("rows", "feat")
    return jax.shard_map(body, mesh=mesh, in_specs=in_specs, out_specs=out_specs, check_vma=False)
```

```python
import math
import jax
import jax.numpy as jnp
from jax import lax
from jax.experimental import pallas as pl
from jax.experimental.pallas import tpu as pltpu
from jax.sharding import PartitionSpec as P

NORM_EPS = 1e-06
VAR_EPS = 1e-05

NZ, NR, NF, NY = 16, 64, 8, 4
QB = 16
CHUNKS = 8
LANES = 128
KINDS = "YYYYyxxx"
MESH = pl.DeviceIdType.MESH
EARLY = (0, 1)
SCHEDULE = [(3, 0), (2, 4), (3, 1), (2, 5), (3, 2), (2, 6), (3, 3), (2, 7), (3, 4), (3, 5), (3, 6), (3, 7)]
SCHEDULE += [(4, i) for i in range(CHUNKS)]


FIRST, SECOND = (3, -3, 1, -1), (6, -6)
THIRD, LAST = (4, -4, 2, -2), (7, -7, 5, -5, 8)


def kernel(
    g_hbm, q_hbm, lw_hbm, o_ref,
    g, qall, lw, part, y_got, y_out, own, x_out, x_got,
    sq_mine, sq_got, sq_pair, sq_far, factor, turned, scored, stat_mine, stat_got,
    l_sem, o_sem, z_recv, x_recv, c_recv, y_recv, p_recv, s_recv, t_recv,
):
    r, f = lax.axis_index("rows"), lax.axis_index("feat")
    z, xh, c = r // 4, lax.rem(r // 2, 2), lax.rem(r, 2)
    y, xl = f // 2, lax.rem(f, 2)
    rows, cols = g.shape
    size = rows // 2
    portion = qall.shape[0] // 4
    per = portion // NF

    def at(dz, xh_to, c_to):
        return (lax.rem(z + dz + NZ, NZ) * 4 + xh_to * 2 + c_to, f)

    def y_peer(k):
        return (r, lax.rem(y + k, NY) * 2 + xl)

    x_peer = (r, y * 2 + 1 - xl)

    def block(dz, xh_of, c_of):
        first = (xh_of * 2 + c_of) * portion + lax.rem(z + dz + NZ, NZ) * QB
        return qall.at[pl.ds(pl.multiple_of(first, QB), QB)]

    def whole(xh_of, c_of):
        first = (xh_of * 2 + c_of) * portion
        return qall.at[pl.ds(pl.multiple_of(first, portion), portion)]

    loads = [
        pltpu.make_async_copy(q_hbm, block(0, xh, c), l_sem.at[0]),
        pltpu.make_async_copy(g_hbm, g, l_sem.at[1]),
        pltpu.make_async_copy(lw_hbm, lw, l_sem.at[2]),
    ]
    for load in loads:
        load.start()

    barrier = pltpu.get_barrier_semaphore()
    greet = [at(d, xh, c) for d in (3, -3, 4 * c - 2, 1, -1)]
    greet += [at(0, 1 - xh, c), at(0, xh, 1 - c), x_peer]
    greet += [y_peer(k) for k in range(1, NY)]
    for device in greet:
        pl.semaphore_signal(barrier, inc=1, device_id=device, device_id_type=MESH)
    loads[0].wait()
    pl.semaphore_wait(barrier, len(greet))

    sent = [0, 0, 0]

    def push(src, dst, group, rsem, device):
        pltpu.make_async_remote_copy(
            src_ref=src, dst_ref=dst, send_sem=o_sem.at[group], recv_sem=rsem,
            device_id=device, device_id_type=MESH).start()
        if group < 3:
            sent[group] += math.prod(src.shape) // cols

    def waiter(ref, ssem, rsem):
        return pltpu.make_async_remote_copy(
            src_ref=ref, dst_ref=ref, send_sem=ssem, recv_sem=rsem,
            device_id=at(0, xh, 1 - c), device_id_type=MESH)

    def landed(dst, rsem):
        waiter(dst, o_sem.at[0], rsem).wait_recv()

    def z_push(d, step):
        here = block(-d, xh, c)
        push(here, here, 0, z_recv.at[(d + step) % NZ], at(step, xh, c))

    def share(d):
        here = block(-d, xh, c)
        push(here, here, 0, x_recv.at[d % NZ], at(0, 1 - xh, c))
        push(here, here, 0, c_recv.at[0], at(0, xh, 1 - c))

    def share_x(ds):
        for d in ds:
            here = block(-d, 1 - xh, c)
            landed(here, x_recv.at[d % NZ])
            push(here, here, 0, c_recv.at[1], at(0, xh, 1 - c))

    for step in (3, -3, 1, -1):
        z_push(0, step)
    share(0)

    loads[1].wait()
    for i in range(rows // LANES):
        sums = jnp.zeros((LANES, LANES), jnp.float32)
        for j in range(cols // LANES):
            v = g[i * LANES:(i + 1) * LANES, j * LANES:(j + 1) * LANES].astype(jnp.float32)
            sums = sums + v * v
        sq_mine[:, i * LANES:(i + 1) * LANES] = jnp.sum(jnp.transpose(sums), axis=0, keepdims=True)
    for k in range(1, NY):
        push(sq_mine, sq_got.at[k - 1], 3, s_recv.at[0], y_peer(k))

    for d in FIRST:
        landed(block(-d, xh, c), z_recv.at[d % NZ])
        if abs(d) == 3:
            z_push(d, d)
            if d == -3:
                for near in (3, -3):
                    for step in (1, -1):
                        z_push(near, step)
        share(d)
    share_x((0,))
    for d in SECOND:
        landed(block(-d, xh, c), z_recv.at[d % NZ])
        z_push(d, 1)
        z_push(d, -1)
        if d == -6:
            turn = 1 - 2 * c
            here = block(-6 * turn, xh, c)
            push(here, here, 0, z_recv.at[8], at(2 * turn, xh, c))
        share(d)
    share_x(FIRST[:2])
    for d in THIRD:
        landed(block(-d, xh, c), z_recv.at[d % NZ])
        share(d)

    total = sq_mine[...]
    landed(sq_got, s_recv.at[0])
    for k in range(1, NY):
        total = total + sq_got[k - 1]
    sq_pair[...] = total
    push(sq_pair, sq_far, 4, s_recv.at[1], x_peer)
    share_x(FIRST[2:])

    for d in LAST:
        landed(block(-d, xh, c), z_recv.at[d % NZ])
        share(d)
    def y_row(k):
        return lax.rem(y + k + NY, NY)

    def source(i):
        return (xh if i < 4 else 1 - xh), (c if i % 4 < 2 else 1 - c)

    def span(i):
        return slice(i % 2 * size, (i % 2 + 1) * size)

    def y_push(i, src, slot, wide, k):
        dst = y_got.at[i, slot] if wide else y_got.at[i, slot, 0]
        alone = slot == 1 and KINDS[i] in "YX"
        push(src, dst, 1, y_recv.at[i, int(alone)], y_peer(k % NY))

    def y_wait(i, alone=False):
        if alone:
            ref = y_got.at[i, 1]
        else:
            ref = y_got.at[i, 0:2] if KINDS[i] in "YX" else y_got.at[i]
        if KINDS[i] in "Xx":
            ref = ref.at[0] if alone else ref.at[:, 0]
        landed(ref, y_recv.at[i, int(alone)])

    def sign(i):
        return 1 if i % 2 == 0 else -1

    def wide_part(i, k):
        return part.at[i, pl.ds(y_row(k) * 2, 2)]

    def multiply(i):
        value = lax.dot_general(
            whole(*source(i))[...], g[span(i), :],
            (((1,), (1,)), ((), ())), preferred_element_type=jnp.float32)
        y_first = KINDS[i] in "Yy"
        for b in range(NF):
            part[i, b if y_first else b % 2 * NY + b // 2] = value[b * per:(b + 1) * per].astype(jnp.bfloat16)
        s = sign(i)
        if KINDS[i] == "Y":
            y_push(i, wide_part(i, 2), 1, True, s)
            y_push(i, wide_part(i, -s), 0, True, -s)
        elif KINDS[i] == "y":
            for k in (2, 1, 3):
                y_push(i, wide_part(i, k), k - 1, True, k)
        else:
            push(part.at[i, pl.ds((1 - xl) * NY, NY)], x_got.at[i], 2, p_recv.at[i], x_peer)

    def second(i):
        s = sign(i)
        if KINDS[i] == "Y":
            y_wait(i, True)
            both = wide_part(i, s)[...].astype(jnp.float32) + y_got[i, 1].astype(jnp.float32)
            y_out[i, 0:2] = both.astype(jnp.bfloat16)
            y_push(i, y_out.at[i, 0:2], 2, True, s)
        elif KINDS[i] in "Xx":
            landed(x_got.at[i], p_recv.at[i])
            for k in (2, 1, 3, 0):
                to = y_row(k)
                both = part[i, xl * NY + to].astype(jnp.float32) + x_got[i, to].astype(jnp.float32)
                if k == 0:
                    own[i] = both
                    continue
                y_out[i, k - 1] = both.astype(jnp.bfloat16)
                if KINDS[i] == "x":
                    y_push(i, y_out.at[i, k - 1], k - 1, False, k)
                elif k == 2:
                    y_push(i, y_out.at[i, 1], 1, False, s)
                elif k == -s % NY:
                    y_push(i, y_out.at[i, k - 1], 0, False, -s)

    def third(i):
        s = sign(i)
        if KINDS[i] in "Yy":
            near = part[i, y * 2 + xl].astype(jnp.float32)
            far = part[i, y * 2 + 1 - xl].astype(jnp.float32)
            y_wait(i)
            for slot in (0, 2) if KINDS[i] == "Y" else (0, 1, 2):
                near = near + y_got[i, slot, xl].astype(jnp.float32)
                far = far + y_got[i, slot, 1 - xl].astype(jnp.float32)
            own[i] = near
            x_out[i] = far.astype(jnp.bfloat16)
            push(x_out.at[i], x_got.at[i, 0], 2, p_recv.at[i], x_peer)
        elif KINDS[i] == "X":
            y_wait(i, True)
            mine = s % NY - 1
            both = y_out[i, mine].astype(jnp.float32) + y_got[i, 1, 0].astype(jnp.float32)
            y_out[i, 3] = both.astype(jnp.bfloat16)
            y_push(i, y_out.at[i, 3], 2, False, s)

    def finish(i):
        raw = own[i]
        if KINDS[i] in "Yy":
            landed(x_got.at[i, 0], p_recv.at[i])
            raw = raw + x_got[i, 0].astype(jnp.float32)
        else:
            y_wait(i)
            for slot in (0, 2) if KINDS[i] == "X" else (0, 1, 2):
                raw = raw + y_got[i, slot, 0].astype(jnp.float32)
        raw = raw * factor[:, span(i)]
        xh_of, c_of = source(i)
        for low in range(per // QB):
            first = low * (4 * QB) + (xh_of * 2 + c_of) * QB
            turned[pl.ds(pl.multiple_of(first, QB), QB), span(i)] = raw[low * QB:(low + 1) * QB]

    def turn(h):
        value = jnp.transpose(turned[:, h * size:(h + 1) * size])
        scored[h * size:(h + 1) * size, :] = value
        return jnp.sum(value, axis=0, keepdims=True)

    multiply(0)
    multiply(1)
    share_x(SECOND)
    landed(whole(xh, 1 - c), c_recv.at[0])
    multiply(2)
    multiply(3)
    share_x(THIRD)
    share_x(LAST)
    multiply(5)
    multiply(4)
    for i in EARLY:
        second(i)
    landed(whole(1 - xh, 1 - c), c_recv.at[1])
    multiply(6)
    multiply(7)
    landed(sq_far, s_recv.at[1])
    loads[2].wait()
    factor[...] = lw[...] / jnp.sqrt((sq_pair[...] + sq_far[...]) / (cols * NF) + NORM_EPS)
    for i in range(4):
        if i not in EARLY:
            second(i)
    for step, i in SCHEDULE:
        (second, third, finish)[step - 2](i)
    column_sum = turn(0) + turn(1)
    own_mean = column_sum / rows
    off = scored[...] - own_mean
    stat_mine[0:1, :] = own_mean
    stat_mine[1:2, :] = jnp.sum(off * off, axis=0, keepdims=True)

    for i in sorted(range(1, NR), key=lambda i: abs(i - NR // 2)):
        push(stat_mine, stat_got.at[i - 1], 5, t_recv, (lax.rem(r + i, NR), f))
    for group, count in enumerate(sent):
        waiter(qall.at[pl.ds(0, count)], o_sem.at[group], t_recv).wait_send()
    waiter(sq_got, o_sem.at[3], t_recv).wait_send()
    waiter(sq_far, o_sem.at[4], t_recv).wait_send()
    stat_wait = waiter(stat_got, o_sem.at[5], t_recv)
    stat_wait.wait_recv()

    means = stat_got[:, 0, :]
    mean = (jnp.sum(means, axis=0, keepdims=True) + own_mean) / NR
    apart = means - mean
    own_apart = own_mean - mean
    spread = jnp.sum(stat_got[:, 1, :], axis=0, keepdims=True) + stat_mine[1:2, :]
    spread = spread + rows * (jnp.sum(apart * apart, axis=0, keepdims=True) + own_apart * own_apart)
    scale = lax.rsqrt(spread / (rows * NR) + VAR_EPS)
    o_ref[...] = ((scored[...] - mean) * scale).astype(o_ref.dtype)
    stat_wait.wait_send()


def body(gradients, queries, loss_weight):
    rows, cols = gradients.shape
    width = queries.shape[0] * NR // NF
    per, size = width // 4, rows // 2
    half, f32 = jnp.bfloat16, jnp.float32
    vmem, dma = pltpu.VMEM, pltpu.SemaphoreType.DMA
    return pl.pallas_call(
        kernel,
        out_shape=jax.ShapeDtypeStruct((rows, width), jnp.bfloat16),
        in_specs=[pl.BlockSpec(memory_space=pltpu.HBM)] * 3,
        out_specs=pl.BlockSpec(memory_space=pltpu.VMEM),
        scratch_shapes=[
            vmem((rows, cols), half),
            vmem((NR * QB, cols), half),
            vmem((1, rows), f32),
            vmem((CHUNKS, NF, per, size), half),
            vmem((CHUNKS, NY - 1, 2, per, size), half),
            vmem((CHUNKS, NY, per, size), half),
            vmem((CHUNKS, per, size), f32),
            vmem((CHUNKS, per, size), half),
            vmem((CHUNKS, NY, per, size), half),
            vmem((1, rows), f32),
            vmem((NY - 1, 1, rows), f32),
            vmem((1, rows), f32),
            vmem((1, rows), f32),
            vmem((1, rows), f32),
            vmem((width, rows), f32),
            vmem((rows, width), f32),
            vmem((2, width), f32),
            vmem((NR - 1, 2, width), f32),
            dma((3,)), dma((6,)), dma((NZ,)), dma((NZ,)), dma((2,)),
            dma((CHUNKS, 2)), dma((CHUNKS,)), dma((2,)), dma,
        ],
        compiler_params=pltpu.CompilerParams(
            collective_id=0, has_side_effects=True, vmem_limit_bytes=48 * 2**20),
        cost_estimate=pl.CostEstimate(
            flops=2 * rows * NR * QB * cols, bytes_accessed=2 * rows * (cols + width), transcendentals=0),
        name="scores",
    )(*(pltpu.with_memory_space_constraint(v, pltpu.HBM) for v in (gradients, queries, loss_weight.reshape(1, rows))))


def solution(mesh):
    in_specs = (P("rows", "feat"), P("rows", "feat"), P("rows"))
    out_specs = P("rows", "feat")
    return jax.shard_map(body, mesh=mesh, in_specs=in_specs, out_specs=out_specs, check_vma=False)
```
